32 devices in a mesh: gx: 4 (over y, core), gy: 4 (over z), gz: 2 (over x).
Axes of the slice: x: 2, y: 2, z: 4, core: 2. Of those that a mesh axis runs over, the one named last changes fastest.
Arguments:
- tokens: bfloat16 [512, 8192], P('gx', ('gz', 'gy')), may hold values from -6 to 6
- gate_weight: bfloat16 [14336, 8192], P(('gy', 'gx'), 'gz'), may hold values from -0.0625 to 0.0625
- up_weight: bfloat16 [14336, 8192], P(('gy', 'gx'), 'gz'), may hold values from -0.0625 to 0.0625
- down_weight: bfloat16 [14336, 8192], P(('gy', 'gx'), 'gz'), may hold values from -0.046875 to 0.046875
- reward_head: bfloat16 [8192], P(('gz', 'gy')), may hold values from -0.0625 to 0.0625
- lm_grad: float32 [512, 8192], P('gx', ('gz', 'gy')), may hold values from -6 to 6
- pair_index: int32 [2, 2], replicated, may hold values from 0 to 3, as said below
Outputs:
- grad_tokens: float32 [512, 8192], P('gx', ('gz', 'gy'))
- grad_gate: float32 [14336, 8192], P(('gy', 'gx'), 'gz')
- grad_up: float32 [14336, 8192], P(('gy', 'gx'), 'gz')
- grad_down: float32 [14336, 8192], P(('gy', 'gx'), 'gz')
- rewards: float32 [4], replicated
The draws below stay inside these ranges and needn't reach their ends.
Inputs may be any that keep to these rules, and one draw needn't show every extreme that they name: Every sequence number of 0 to 3 stands exactly once in pair_index.
All inputs are finite; a program needn't handle non-finite values.
Results may differ from the reference program's by a relative error of at most 0.008.
Values may be sent and summed in bfloat16 or wider, within the bound.
A program may use at most 256 MiB of HBM per device.

```python
import jax
import jax.numpy as jnp
from jax import lax

D = 8192
FF = 14336
SEQ_LEN = 128
TOKENS = 512
SEQS = 4
PAIRS = 2


def draw_pair_index(key, part):
    key = jax.random.fold_in(key, 7)
    order = jax.random.permutation(key, SEQS)
    return order.reshape(PAIRS, 2).astype(jnp.int32)


def levels(stream_key, dims, split, smallest, high):
    def one(axis_at, parts):
        draws = jax.random.uniform(jax.random.fold_in(jax.random.fold_in(stream_key, 6), axis_at), (parts,), jnp.float32, smallest / len(split), high / len(split))
        return jnp.repeat(jnp.exp(draws), dims[axis_at] // parts).reshape((-1,) + (1,) * (len(dims) - axis_at - 1))

    level = one(*split[0])
    for cut in split[1:]:
        level = level * one(*cut)
    return level


def normal_values(key, dims, scale, reach, split=(), held_as=jnp.bfloat16):
    array = jax.random.normal(key, dims, jnp.float32) * scale
    if len(split) > 0:
        array = levels(key, dims, split, -0.22, 0.18) * array
    return jnp.clip(array, min=-reach, max=reach).astype(held_as)


def setup_inputs(seed: int = 0) -> dict:
    streams_of = jax.random.split(jax.random.key(seed), 8)
    return {
        "tokens": normal_values(streams_of[0], (TOKENS, D), 1.0, 6.0, ((0, 4), (1, 8))),
        "gate_weight": normal_values(streams_of[1], (FF, D), D ** -0.5, 0.0625, ((0, 16), (1, 2))),
        "up_weight": normal_values(streams_of[2], (FF, D), D ** -0.5, 0.0625, ((0, 16), (1, 2))),
        "down_weight": normal_values(streams_of[3], (FF, D), FF ** -0.5, 0.046875, ((0, 16), (1, 2))),
        "reward_head": normal_values(streams_of[4], (D,), D ** -0.5, 0.0625, ((0, 8),)),
        "lm_grad": normal_values(streams_of[5], (TOKENS, D), 1.0, 6.0, ((0, 4), (1, 8)), jnp.float32),
        "pair_index": draw_pair_index(jax.random.fold_in(streams_of[7], 71), 0),
    }


reward_weight = 64.0

def reference(tokens, gate_weight, up_weight, down_weight, reward_head, lm_grad, pair_index):
    gate_sum = jnp.dot(tokens, gate_weight.T, preferred_element_type=jnp.float32)
    up_sum = jnp.dot(tokens, up_weight.T, preferred_element_type=jnp.float32)
    gate_sigmoid = jax.nn.sigmoid(gate_sum)
    silu_gate = gate_sum * gate_sigmoid
    hidden = (silu_gate * up_sum).astype(jnp.bfloat16)
    ffn_out = jnp.dot(hidden, down_weight, preferred_element_type=jnp.float32)
    block_out = tokens.astype(jnp.float32) + ffn_out
    head_vec = reward_head.astype(jnp.float32)
    last_rows = block_out.reshape(SEQS, SEQ_LEN, D)[:, SEQ_LEN - 1, :]
    rewards = lax.optimization_barrier(jnp.sum(last_rows * head_vec[None, :], axis=1))
    sequence = jnp.arange(SEQS, dtype=jnp.int32)
    chosen_hot = (pair_index[:, 0:1] == sequence[None, :]).astype(jnp.float32)
    rejected_hot = (pair_index[:, 1:2] == sequence[None, :]).astype(jnp.float32)
    margin = lax.optimization_barrier(jnp.sum(chosen_hot * rewards[None, :], axis=1)) - lax.optimization_barrier(jnp.sum(rejected_hot * rewards[None, :], axis=1))
    pair_weight = jax.nn.sigmoid(-margin)
    pair_coefs = lax.optimization_barrier(jnp.sum((rejected_hot - chosen_hot) * pair_weight[:, None], axis=0))
    head_term = reward_weight * pair_coefs[:, None] * head_vec[None, :]
    grad_out = lm_grad.reshape(SEQS, SEQ_LEN, D).at[:, SEQ_LEN - 1, :].add(head_term).reshape(TOKENS, D)
    grad_low = grad_out.astype(jnp.bfloat16)
    hidden_grad = jnp.dot(grad_low, down_weight.T, preferred_element_type=jnp.float32)
    up_grad = (hidden_grad * silu_gate).astype(jnp.bfloat16)
    gate_grad = (hidden_grad * up_sum * gate_sigmoid * (1.0 + gate_sum * (1.0 - gate_sigmoid))).astype(jnp.bfloat16)
    grad_tokens = grad_out + jnp.dot(gate_grad, gate_weight, preferred_element_type=jnp.float32) + jnp.dot(up_grad, up_weight, preferred_element_type=jnp.float32)
    loss_scale = 1.0 / jnp.sqrt(jnp.float32(TOKENS))
    grad_gate = jnp.dot(gate_grad.T, tokens, preferred_element_type=jnp.float32) * loss_scale
    grad_up = jnp.dot(up_grad.T, tokens, preferred_element_type=jnp.float32) * loss_scale
    grad_down = jnp.dot(hidden.T, grad_low, preferred_element_type=jnp.float32) * loss_scale
    return (grad_tokens, grad_gate, grad_up, grad_down, rewards)
```

```python
import jax
import jax.numpy as jnp
from jax import lax
from jax.sharding import PartitionSpec as P

SEQ_LEN = 128


reward_weight = 64.0


def swap(value, axis, bit):
    size = lax.axis_size(axis)
    return lax.ppermute(value, axis, [(i, i ^ bit) for i in range(size)])


def bits_down(axis):
    bit = lax.axis_size(axis) // 2
    bits = []
    while bit >= 1:
        bits.append(bit)
        bit //= 2
    return bits


def gx_offsets():
    offsets = [0]
    for bit in bits_down("gx"):
        offsets = offsets + [offset ^ bit for offset in offsets]
    return offsets


def ordered_features(pieces):
    me = lax.axis_index("gy")
    stacked = jnp.stack(pieces)
    return jnp.concatenate(
        [lax.dynamic_index_in_dim(stacked, me ^ p, 0, keepdims=False) for p in range(len(pieces))],
        axis=-1,
    )


def gather_halves(shard):
    pieces = [[shard] + [swap(shard, "gy", j) for j in range(1, lax.axis_size("gy"))]]
    for bit in bits_down("gx")[:-1]:
        pieces = pieces + [[swap(piece, "gx", bit) for piece in row] for row in pieces]
    first = jnp.concatenate([ordered_features(row) for row in pieces], axis=0)
    return first, swap(first, "gx", 1)


def right_product(left, right):
    return lax.dot_general(
        left, right, (((1,), (1,)), ((), ())), preferred_element_type=jnp.float32
    )


def feature_sum(partial_value):
    size = lax.axis_size("gz")
    low = partial_value.astype(jnp.bfloat16)
    total = partial_value
    for j in range(1, size):
        total = total + swap(low, "gz", j).astype(jnp.float32)
    return total


def sum_all(value):
    for axis in ("gz", "gx", "gy"):
        for bit in bits_down(axis):
            value = value + swap(value, axis, bit)
    return value


def body(tokens, gate_weight, up_weight, down_weight, reward_head, lm_grad, pair_index):
    row_count, feature_count = tokens.shape
    seq_dev = row_count // SEQ_LEN
    gx_size = lax.axis_size("gx")
    gy_size = lax.axis_size("gy")
    seq_total = seq_dev * gx_size
    me = lax.axis_index("gx")
    offsets = gx_offsets()

    tok_halves = gather_halves(tokens)
    low_halves = gather_halves(lm_grad.astype(jnp.bfloat16))
    head_own = reward_head.astype(jnp.float32)
    head_block = ordered_features(
        [reward_head] + [swap(reward_head, "gy", j) for j in range(1, gy_size)]
    )
    head_wide = jnp.broadcast_to(head_block[None, :], (8, head_block.shape[0]))
    head_part = right_product(head_wide, down_weight)[0]
    head_sum = head_part
    for j in range(1, lax.axis_size("gz")):
        head_sum = head_sum + swap(head_part, "gz", j)

    gate_halves = [feature_sum(right_product(half, gate_weight)) for half in tok_halves]
    up_halves = [feature_sum(right_product(half, up_weight)) for half in tok_halves]
    base_halves = [feature_sum(right_product(half, down_weight)) for half in low_halves]

    gate_sum = jnp.concatenate(gate_halves, axis=0)
    up_sum = jnp.concatenate(up_halves, axis=0)
    hidden_base = jnp.concatenate(base_halves, axis=0)
    tok_all = jnp.concatenate(tok_halves, axis=0)
    low_all = jnp.concatenate(low_halves, axis=0)
    unit_count = gate_sum.shape[1]

    gate_sigmoid = jax.nn.sigmoid(gate_sum)
    silu_gate = gate_sum * gate_sigmoid
    hidden = (silu_gate * up_sum).astype(jnp.bfloat16)

    last_hidden = hidden.reshape(seq_total, SEQ_LEN, unit_count)[:, SEQ_LEN - 1, :]
    last_terms = jnp.sum(last_hidden.astype(jnp.float32) * head_part[None, :], axis=1)
    last_tokens = tokens.reshape(seq_dev, SEQ_LEN, feature_count)[:, SEQ_LEN - 1, :]
    own_terms = jnp.sum(last_tokens.astype(jnp.float32) * head_own[None, :], axis=1)
    place = (me ^ jnp.array(offsets, jnp.int32))[:, None] * seq_dev + jnp.arange(seq_dev)[None, :]
    place = place.reshape(-1)
    one_hot = (place[:, None] == jnp.arange(seq_total)[None, :]).astype(jnp.float32)
    local_terms = last_terms.at[:seq_dev].add(own_terms)
    rewards = sum_all(jnp.sum(one_hot * local_terms[:, None], axis=0))

    sequence = jnp.arange(seq_total, dtype=jnp.int32)
    chosen_hot = (pair_index[:, 0:1] == sequence[None, :]).astype(jnp.float32)
    rejected_hot = (pair_index[:, 1:2] == sequence[None, :]).astype(jnp.float32)
    margin = jnp.sum(chosen_hot * rewards[None, :], axis=1) - jnp.sum(
        rejected_hot * rewards[None, :], axis=1
    )
    pair_weight = jax.nn.sigmoid(-margin)
    pair_coefs = jnp.sum((rejected_hot - chosen_hot) * pair_weight[:, None], axis=0)
    coefs = reward_weight * jnp.sum(one_hot * pair_coefs[None, :], axis=1)

    def with_last(value, vector, scales):
        count = scales.shape[0]
        is_last = (jnp.arange(SEQ_LEN) == SEQ_LEN - 1).astype(jnp.float32)
        rows = (scales[:, None] * is_last[None, :]).reshape(count * SEQ_LEN)
        return value + rows[:, None] * vector[None, :]

    hidden_grad = with_last(hidden_base, head_sum, coefs)
    up_grad = (hidden_grad * silu_gate).astype(jnp.bfloat16)
    gate_grad = (
        hidden_grad * up_sum * gate_sigmoid * (1.0 + gate_sum * (1.0 - gate_sigmoid))
    ).astype(jnp.bfloat16)

    token_part = jnp.dot(gate_grad, gate_weight, preferred_element_type=jnp.float32) + jnp.dot(
        up_grad, up_weight, preferred_element_type=jnp.float32
    )
    for bit in reversed(bits_down("gx")):
        half = token_part.shape[0] // 2
        sent = token_part[half:].astype(jnp.bfloat16)
        token_part = token_part[:half] + swap(sent, "gx", bit).astype(jnp.float32)
    blocks = token_part.reshape(row_count, gy_size, feature_count)
    gy_me = lax.axis_index("gy")
    token_sum = lax.dynamic_index_in_dim(blocks, gy_me, 1, keepdims=False)
    for j in range(1, gy_size):
        sent = lax.dynamic_index_in_dim(blocks, gy_me ^ j, 1, keepdims=False)
        token_sum = token_sum + swap(sent.astype(jnp.bfloat16), "gy", j).astype(jnp.float32)
    grad_tokens = with_last(lm_grad, head_own, coefs[:seq_dev]) + token_sum

    grad_low = with_last(
        low_all.astype(jnp.float32), head_block.astype(jnp.float32), coefs
    ).astype(jnp.bfloat16)
    loss_scale = 1.0 / jnp.sqrt(jnp.float32(row_count * gx_size))

    def weight_grad(left, right):
        return jnp.einsum("tf,td->fd", left, right, preferred_element_type=jnp.float32) * loss_scale

    return (
        grad_tokens,
        weight_grad(gate_grad, tok_all),
        weight_grad(up_grad, tok_all),
        weight_grad(hidden, grad_low),
        rewards,
    )


def solution(mesh):
    placed = (
        P("gx", ("gz", "gy")),
        P(("gy", "gx"), "gz"),
        P(("gy", "gx"), "gz"),
        P(("gy", "gx"), "gz"),
        P(("gz", "gy")),
        P("gx", ("gz", "gy")),
        P(),
    )
    return jax.shard_map(
        body,
        mesh=mesh,
        in_specs=placed,
        out_specs=(
            P("gx", ("gz", "gy")),
            P(("gy", "gx"), "gz"),
            P(("gy", "gx"), "gz"),
            P(("gy", "gx"), "gz"),
            P(),
        ),
        check_vma=False,
    )
```

```python
import jax
import jax.numpy as jnp
from jax import lax
from jax.experimental import pallas as pl
from jax.experimental.pallas import tpu as pltpu
from jax.sharding import PartitionSpec as P

SEQ_LEN = 128


reward_weight = 64.0


def swap(value, axis, bit):
    size = lax.axis_size(axis)
    return lax.ppermute(value, axis, [(i, i ^ bit) for i in range(size)])


def bits_down(axis):
    bit = lax.axis_size(axis) // 2
    bits = []
    while bit >= 1:
        bits.append(bit)
        bit //= 2
    return bits


def gx_offsets():
    offsets = [0]
    for bit in bits_down("gx"):
        offsets = offsets + [offset ^ bit for offset in offsets]
    return offsets


def ordered_features(pieces):
    me = lax.axis_index("gy")
    stacked = jnp.stack(pieces)
    return jnp.concatenate(
        [lax.dynamic_index_in_dim(stacked, me ^ p, 0, keepdims=False) for p in range(len(pieces))],
        axis=-1,
    )


def gather_halves(shard):
    pieces = [[shard] + [swap(shard, "gy", j) for j in range(1, lax.axis_size("gy"))]]
    for bit in bits_down("gx")[:-1]:
        pieces = pieces + [[swap(piece, "gx", bit) for piece in row] for row in pieces]
    first = jnp.concatenate([ordered_features(row) for row in pieces], axis=0)
    return first, swap(first, "gx", 1)


def right_product(left, right):
    return lax.dot_general(
        left, right, (((1,), (1,)), ((), ())), preferred_element_type=jnp.float32
    )


def feature_sum(partial_value):
    size = lax.axis_size("gz")
    low = partial_value.astype(jnp.bfloat16)
    total = partial_value
    for j in range(1, size):
        total = total + swap(low, "gz", j).astype(jnp.float32)
    return total


def sum_all(value):
    for axis in ("gz", "gx", "gy"):
        for bit in bits_down(axis):
            value = value + swap(value, axis, bit)
    return value


def permute_body(tokens, gate_weight, up_weight, down_weight, reward_head, lm_grad, pair_index):
    row_count, feature_count = tokens.shape
    seq_dev = row_count // SEQ_LEN
    gx_size = lax.axis_size("gx")
    gy_size = lax.axis_size("gy")
    seq_total = seq_dev * gx_size
    me = lax.axis_index("gx")
    offsets = gx_offsets()

    tok_halves = gather_halves(tokens)
    low_halves = gather_halves(lm_grad.astype(jnp.bfloat16))
    head_own = reward_head.astype(jnp.float32)
    head_block = ordered_features(
        [reward_head] + [swap(reward_head, "gy", j) for j in range(1, gy_size)]
    )
    head_wide = jnp.broadcast_to(head_block[None, :], (8, head_block.shape[0]))
    head_part = right_product(head_wide, down_weight)[0]
    head_sum = head_part
    for j in range(1, lax.axis_size("gz")):
        head_sum = head_sum + swap(head_part, "gz", j)

    gate_halves = [feature_sum(right_product(half, gate_weight)) for half in tok_halves]
    up_halves = [feature_sum(right_product(half, up_weight)) for half in tok_halves]
    base_halves = [feature_sum(right_product(half, down_weight)) for half in low_halves]

    gate_sum = jnp.concatenate(gate_halves, axis=0)
    up_sum = jnp.concatenate(up_halves, axis=0)
    hidden_base = jnp.concatenate(base_halves, axis=0)
    tok_all = jnp.concatenate(tok_halves, axis=0)
    low_all = jnp.concatenate(low_halves, axis=0)
    unit_count = gate_sum.shape[1]

    gate_sigmoid = jax.nn.sigmoid(gate_sum)
    silu_gate = gate_sum * gate_sigmoid
    hidden = (silu_gate * up_sum).astype(jnp.bfloat16)

    last_hidden = hidden.reshape(seq_total, SEQ_LEN, unit_count)[:, SEQ_LEN - 1, :]
    last_terms = jnp.sum(last_hidden.astype(jnp.float32) * head_part[None, :], axis=1)
    last_tokens = tokens.reshape(seq_dev, SEQ_LEN, feature_count)[:, SEQ_LEN - 1, :]
    own_terms = jnp.sum(last_tokens.astype(jnp.float32) * head_own[None, :], axis=1)
    place = (me ^ jnp.array(offsets, jnp.int32))[:, None] * seq_dev + jnp.arange(seq_dev)[None, :]
    place = place.reshape(-1)
    one_hot = (place[:, None] == jnp.arange(seq_total)[None, :]).astype(jnp.float32)
    local_terms = last_terms.at[:seq_dev].add(own_terms)
    rewards = sum_all(jnp.sum(one_hot * local_terms[:, None], axis=0))

    sequence = jnp.arange(seq_total, dtype=jnp.int32)
    chosen_hot = (pair_index[:, 0:1] == sequence[None, :]).astype(jnp.float32)
    rejected_hot = (pair_index[:, 1:2] == sequence[None, :]).astype(jnp.float32)
    margin = jnp.sum(chosen_hot * rewards[None, :], axis=1) - jnp.sum(
        rejected_hot * rewards[None, :], axis=1
    )
    pair_weight = jax.nn.sigmoid(-margin)
    pair_coefs = jnp.sum((rejected_hot - chosen_hot) * pair_weight[:, None], axis=0)
    coefs = reward_weight * jnp.sum(one_hot * pair_coefs[None, :], axis=1)

    def with_last(value, vector, scales):
        count = scales.shape[0]
        is_last = (jnp.arange(SEQ_LEN) == SEQ_LEN - 1).astype(jnp.float32)
        rows = (scales[:, None] * is_last[None, :]).reshape(count * SEQ_LEN)
        return value + rows[:, None] * vector[None, :]

    hidden_grad = with_last(hidden_base, head_sum, coefs)
    up_grad = (hidden_grad * silu_gate).astype(jnp.bfloat16)
    gate_grad = (
        hidden_grad * up_sum * gate_sigmoid * (1.0 + gate_sum * (1.0 - gate_sigmoid))
    ).astype(jnp.bfloat16)

    token_part = jnp.dot(gate_grad, gate_weight, preferred_element_type=jnp.float32) + jnp.dot(
        up_grad, up_weight, preferred_element_type=jnp.float32
    )
    for bit in reversed(bits_down("gx")):
        half = token_part.shape[0] // 2
        sent = token_part[half:].astype(jnp.bfloat16)
        token_part = token_part[:half] + swap(sent, "gx", bit).astype(jnp.float32)
    blocks = token_part.reshape(row_count, gy_size, feature_count)
    gy_me = lax.axis_index("gy")
    token_sum = lax.dynamic_index_in_dim(blocks, gy_me, 1, keepdims=False)
    for j in range(1, gy_size):
        sent = lax.dynamic_index_in_dim(blocks, gy_me ^ j, 1, keepdims=False)
        token_sum = token_sum + swap(sent.astype(jnp.bfloat16), "gy", j).astype(jnp.float32)
    grad_tokens = with_last(lm_grad, head_own, coefs[:seq_dev]) + token_sum

    grad_low = with_last(
        low_all.astype(jnp.float32), head_block.astype(jnp.float32), coefs
    ).astype(jnp.bfloat16)
    loss_scale = 1.0 / jnp.sqrt(jnp.float32(row_count * gx_size))

    def weight_grad(left, right):
        return jnp.einsum("tf,td->fd", left, right, preferred_element_type=jnp.float32) * loss_scale

    return (
        grad_tokens,
        weight_grad(gate_grad, tok_all),
        weight_grad(up_grad, tok_all),
        weight_grad(hidden, grad_low),
        rewards,
    )


MESH = pl.DeviceIdType.MESH
STRIP = 16


def forward_kernel(
    tok, low, head, gate_hbm, up_hbm, down_hbm, diff,
    tok_out, low_out, hidden_out, gate_grad_out, up_grad_out, reward_out, coef_out,
    weight, tok_all, low_all, head_all, part, sent, got, hidden, gate_grad, up_grad,
    head_part, head_got, terms, terms_got,
    weight_sem, z_send, z_recv, head_send, head_recv, y_send, y_recv, core_send, core_recv,
    x_send, x_recv, v_send, v_recv, r_send, r_recv, out_sem,
):
    rows, width = tok.shape
    units = weight.shape[1]
    me = lax.axis_index("gx")
    z = lax.axis_index("gy")
    x = lax.axis_index("gz")
    core_peer = me + 1 - 2 * lax.rem(me, 2)
    y_peer = lax.rem(me + 2, 4)
    z_from = [z, z + 1 - 2 * lax.rem(z, 2), lax.rem(z + 2, 4), 3 - z]
    chunk_owner = [me, core_peer, y_peer, 3 - me]
    x_peer = 1 - x

    def remote(src, dst, send, recv, **peer):
        return pltpu.make_async_remote_copy(
            src_ref=src, dst_ref=dst, send_sem=send, recv_sem=recv,
            device_id=peer, device_id_type=MESH,
        )

    weight_copies = [
        pltpu.make_async_copy(ref, weight.at[m], weight_sem.at[m])
        for m, ref in enumerate((gate_hbm, up_hbm, down_hbm))
    ]
    for m in (2, 0, 1):
        weight_copies[m].start()

    barrier = pltpu.get_barrier_semaphore()
    peers = [{"gy": z_from[j]} for j in (1, 2, 3)]
    peers += [{"gx": core_peer}, {"gx": y_peer}, {"gz": x_peer}]
    for peer in peers:
        pl.semaphore_signal(barrier, inc=1, device_id=peer, device_id_type=MESH)
    pl.semaphore_wait(barrier, len(peers))

    own = pl.ds(0, rows)
    other = pl.ds(rows, rows)
    pending = []

    def z_copies(a, shard, full):
        sends = [
            remote(shard, full.at[0, z, own], z_send.at[a, j - 1], z_recv.at[a, j - 1], gy=z_from[j])
            for j in (1, 2, 3)
        ]
        recvs = [
            remote(shard, full.at[0, z_from[j], own], z_send.at[a, j - 1], z_recv.at[a, j - 1],
                   gy=z_from[j])
            for j in (1, 2, 3)
        ]
        return sends, recvs

    def y_copies(a, full):
        return [
            remote(full.at[0, z_from[j], own], full.at[1, z_from[j], own],
                   y_send.at[a, j], y_recv.at[a, j], gx=y_peer)
            for j in range(4)
        ]

    def core_copies(a, full):
        return [
            remote(full.at[h, :, own], full.at[h, :, other],
                   core_send.at[a, h], core_recv.at[a, h], gx=core_peer)
            for h in range(2)
        ]

    tok_z, tok_z_recv = z_copies(0, tok, tok_all)
    low_z, low_z_recv = z_copies(1, low, low_all)
    tok_y, low_y = y_copies(0, tok_all), y_copies(1, low_all)
    tok_core, low_core = core_copies(0, tok_all), core_copies(1, low_all)

    head_z = [
        remote(head, head_all.at[z], head_send.at[j - 1], head_recv.at[j - 1], gy=z_from[j])
        for j in (1, 2, 3)
    ]
    head_z_recv = [
        remote(head, head_all.at[z_from[j]], head_send.at[j - 1], head_recv.at[j - 1], gy=z_from[j])
        for j in (1, 2, 3)
    ]
    for copy in head_z + tok_z:
        copy.start()
    tok_all[0, z, 0:rows] = tok[...]
    tok_y[0].start()
    low_all[0, z, 0:rows] = low[...]
    head_all[z] = head[...]
    part[...] = jnp.zeros_like(part)
    head_part[...] = jnp.zeros_like(head_part)

    def columns(k):
        return pl.ds(pl.multiple_of(k * width, width), width)

    def product(full, h, m):
        @pl.loop(0, 4)
        def _(k):
            part[m, h] += lax.dot_general(
                full[h, k], weight[m, :, columns(k)], (((1,), (1,)), ((), ())),
                preferred_element_type=jnp.float32,
            )

        sent[m, h] = part[m, h].astype(jnp.bfloat16)
        x_copies[m][h].start()

    x_copies = [
        [
            remote(sent.at[m, h], got.at[m, h], x_send.at[m, h], x_recv.at[m, h], gz=x_peer)
            for h in range(2)
        ]
        for m in range(3)
    ]

    for copy in head_z_recv:
        copy.wait_recv()
    weight_copies[2].wait()

    @pl.loop(0, 4)
    def _(k):
        head_part[...] += lax.dot_general(
            head_all[k], weight[2, :, columns(k)], (((1,), (1,)), ((), ())),
            preferred_element_type=jnp.float32,
        )

    head_copy = remote(head_part, head_got, v_send, v_recv, gz=x_peer)
    head_copy.start()

    for j in (1, 2, 3):
        tok_z_recv[j - 1].wait_recv()
        tok_y[j].start()
    tok_core[0].start()
    for copy in low_z:
        copy.start()
    weight_copies[0].wait()
    tok_core[0].wait_recv()
    product(tok_all, 0, 0)
    weight_copies[1].wait()
    product(tok_all, 0, 1)

    for copy in tok_y:
        copy.wait_recv()
    tok_core[1].start()
    low_y[0].start()
    tok_core[1].wait_recv()
    tok_stores = [
        pltpu.make_async_copy(
            tok_all.at[:, k], tok_out.at[:, :, pl.ds(k * width, width)], out_sem.at[k]
        )
        for k in range(4)
    ]
    for copy in tok_stores:
        copy.start()
    product(tok_all, 1, 0)
    product(tok_all, 1, 1)

    for j in (1, 2, 3):
        low_z_recv[j - 1].wait_recv()
        low_y[j].start()
    low_core[0].start()
    low_core[0].wait_recv()
    product(low_all, 0, 2)

    def activate(h):
        x_copies[0][h].wait_recv()
        x_copies[1][h].wait_recv()

        @pl.loop(0, 2 * rows // STRIP)
        def _(i):
            strip = pl.ds(pl.multiple_of(i * STRIP, STRIP), STRIP)
            gate_sum = part[0, h, strip] + got[0, h, strip].astype(jnp.float32)
            up_sum = part[1, h, strip] + got[1, h, strip].astype(jnp.float32)
            gate_sigmoid = jax.nn.sigmoid(gate_sum)
            silu_gate = gate_sum * gate_sigmoid
            hidden[h, strip] = (silu_gate * up_sum).astype(jnp.bfloat16)
            part[0, h, strip] = silu_gate
            part[1, h, strip] = up_sum * gate_sigmoid * (1.0 + gate_sum * (1.0 - gate_sigmoid))

    activate(0)
    for copy in low_y:
        copy.wait_recv()
    low_core[1].start()
    low_core[1].wait_recv()
    product(low_all, 1, 2)
    activate(1)
    hidden_store = pltpu.make_async_copy(hidden, hidden_out, out_sem.at[4])
    hidden_store.start()

    lane = lax.broadcasted_iota(jnp.int32, (8, 128), 1)
    last = pl.ds(rows - STRIP, STRIP)
    own_term = jnp.sum(
        tok[last].astype(jnp.float32)[STRIP - 1:] * head[...].astype(jnp.float32)[0:1],
        axis=1, keepdims=True,
    )
    tile = jnp.zeros((8, 128), jnp.float32)
    for c in range(4):
        rows_c = pl.ds((c % 2) * rows + rows - STRIP, STRIP)
        term = jnp.sum(
            hidden[c // 2, rows_c].astype(jnp.float32)[STRIP - 1:] * head_part[0:1],
            axis=1, keepdims=True,
        )
        if c == 0:
            term = term + own_term
        tile = tile + jnp.where(lane == chunk_owner[c], jnp.broadcast_to(term, (8, 128)), 0.0)
    steps = [{"gz": x_peer}, {"gx": core_peer}, {"gx": y_peer}, {"gy": z_from[1]}, {"gy": z_from[2]}]
    for k, peer in enumerate(steps):
        terms[k] = tile
        copy = remote(terms.at[k], terms_got.at[k], r_send.at[k], r_recv.at[k], **peer)
        copy.start()
        copy.wait_recv()
        pending.append(copy)
        tile = tile + terms_got[k]
    reward_out[...] = tile
    pair_weight = jax.nn.sigmoid(jnp.sum(diff[...] * tile, axis=1, keepdims=True))
    coefs = reward_weight * jnp.sum(diff[...] * pair_weight, axis=0, keepdims=True)
    coefs = jnp.broadcast_to(coefs, (8, 128))
    coef_out[...] = coefs
    chunk_coef = [
        jnp.sum(jnp.where(lane == chunk_owner[c], coefs, 0.0), axis=1, keepdims=True)[0:1]
        for c in range(4)
    ]

    row = lax.broadcasted_iota(jnp.int32, (STRIP, 1), 0)

    for copy in low_y + low_core:
        copy.wait_send()
    for c in range(4):
        rows_c = pl.ds((c % 2) * rows + rows - STRIP, STRIP)
        scale = jnp.where(row == STRIP - 1, chunk_coef[c], 0.0)
        for k in range(4):
            value = low_all[c // 2, k, rows_c].astype(jnp.float32)
            value = value + scale * head_all[k].astype(jnp.float32)
            low_all[c // 2, k, rows_c] = value.astype(jnp.bfloat16)
    low_stores = [
        pltpu.make_async_copy(
            low_all.at[:, k], low_out.at[:, :, pl.ds(k * width, width)], out_sem.at[5 + k]
        )
        for k in range(4)
    ]
    for copy in low_stores:
        copy.start()

    head_copy.wait_recv()
    head_sum = head_part[0:1] + head_got[0:1]
    for h in range(2):
        x_copies[2][h].wait_recv()
        for b in range(2):
            coef = chunk_coef[2 * h + b]

            @pl.loop(b * rows // STRIP, (b + 1) * rows // STRIP)
            def _(i):
                strip = pl.ds(pl.multiple_of(i * STRIP, STRIP), STRIP)
                at = row + (i * STRIP - b * rows)
                scale = jnp.where(at == rows - 1, coef, 0.0)
                grad = part[2, h, strip] + got[2, h, strip].astype(jnp.float32)
                grad = grad + scale * head_sum
                up_grad[h, strip] = (grad * part[0, h, strip]).astype(jnp.bfloat16)
                gate_grad[h, strip] = (grad * part[1, h, strip]).astype(jnp.bfloat16)

    stores = [
        pltpu.make_async_copy(gate_grad, gate_grad_out, out_sem.at[9]),
        pltpu.make_async_copy(up_grad, up_grad_out, out_sem.at[10]),
    ]
    for copy in stores:
        copy.start()
    for copy in head_z + tok_z + low_z + tok_y + tok_core + [head_copy] + pending:
        copy.wait_send()
    for copies in x_copies:
        for copy in copies:
            copy.wait_send()
    for copy in tok_stores + low_stores + stores + [hidden_store]:
        copy.wait()


def forward_call(tokens, low, head, gate_weight, up_weight, down_weight, diff):
    rows, width = tokens.shape
    units, features = gate_weight.shape
    low_type, f32 = jnp.bfloat16, jnp.float32
    struct = jax.ShapeDtypeStruct
    vmem = pl.BlockSpec(memory_space=pltpu.VMEM)
    hbm = pl.BlockSpec(memory_space=pl.ANY)
    dma = pltpu.SemaphoreType.DMA
    flops = 6 * 4 * rows * units * features
    return pl.pallas_call(
        forward_kernel,
        out_shape=[
            struct((2, 2 * rows, features), low_type),
            struct((2, 2 * rows, features), low_type),
            struct((2, 2 * rows, units), low_type),
            struct((2, 2 * rows, units), low_type),
            struct((2, 2 * rows, units), low_type),
            struct((8, 128), f32),
            struct((8, 128), f32),
        ],
        in_specs=[vmem, vmem, vmem, hbm, hbm, hbm, vmem],
        out_specs=[hbm, hbm, hbm, hbm, hbm, vmem, vmem],
        scratch_shapes=[
            pltpu.VMEM((3, units, features), low_type),
            pltpu.VMEM((2, 4, 2 * rows, width), low_type),
            pltpu.VMEM((2, 4, 2 * rows, width), low_type),
            pltpu.VMEM((4, 16, width), low_type),
            pltpu.VMEM((3, 2, 2 * rows, units), f32),
            pltpu.VMEM((3, 2, 2 * rows, units), low_type),
            pltpu.VMEM((3, 2, 2 * rows, units), low_type),
            pltpu.VMEM((2, 2 * rows, units), low_type),
            pltpu.VMEM((2, 2 * rows, units), low_type),
            pltpu.VMEM((2, 2 * rows, units), low_type),
            pltpu.VMEM((16, units), f32),
            pltpu.VMEM((16, units), f32),
            pltpu.VMEM((5, 8, 128), f32),
            pltpu.VMEM((5, 8, 128), f32),
            dma((3,)), dma((2, 3)), dma((2, 3)), dma((3,)), dma((3,)),
            dma((2, 4)), dma((2, 4)), dma((2, 2)), dma((2, 2)),
            dma((3, 2)), dma((3, 2)), dma(()), dma(()), dma((5,)), dma((5,)), dma((11,)),
        ],
        compiler_params=pltpu.CompilerParams(
            collective_id=0, has_side_effects=True, vmem_limit_bytes=58 * 1024 * 1024
        ),
        cost_estimate=pl.CostEstimate(
            flops=flops, bytes_accessed=3 * units * features * 2, transcendentals=0
        ),
    )(tokens, low, head, gate_weight, up_weight, down_weight, diff)


def kernel_body(tokens, gate_weight, up_weight, down_weight, reward_head, lm_grad, pair_index):
    rows, width = tokens.shape
    units, features = gate_weight.shape
    me = lax.axis_index("gx")
    seq_total = lax.axis_size("gx")
    sequence = jnp.arange(128, dtype=jnp.int32)
    diff = (pair_index[:, 1:2] == sequence[None, :]).astype(jnp.float32) - (
        pair_index[:, 0:1] == sequence[None, :]
    ).astype(jnp.float32)
    diff = jnp.pad(diff, ((0, 8 - diff.shape[0]), (0, 0)))
    head = jnp.broadcast_to(reward_head[None, :], (16, width))
    tok_all, low_all, hidden, gate_grad, up_grad, reward_tile, coef_tile = forward_call(
        tokens, lm_grad.astype(jnp.bfloat16), head, gate_weight, up_weight, down_weight, diff
    )
    tok_all = tok_all.reshape(4 * rows, features)
    low_all = low_all.reshape(4 * rows, features)
    hidden = hidden.reshape(4 * rows, units)
    gate_grad = gate_grad.reshape(4 * rows, units)
    up_grad = up_grad.reshape(4 * rows, units)
    own_coef = lax.dynamic_index_in_dim(coef_tile[0], me, 0, keepdims=False)

    def token_product(chunk):
        gate_rows = lax.slice_in_dim(gate_grad.reshape(2, 2, rows, units), chunk, chunk + 1, axis=1)
        up_rows = lax.slice_in_dim(up_grad.reshape(2, 2, rows, units), chunk, chunk + 1, axis=1)
        return jnp.dot(
            gate_rows.reshape(2 * rows, units), gate_weight, preferred_element_type=jnp.float32
        ) + jnp.dot(up_rows.reshape(2 * rows, units), up_weight, preferred_element_type=jnp.float32)

    far = swap(token_product(1).astype(jnp.bfloat16), "gx", 1)
    near = token_product(0) + far.astype(jnp.float32)
    y_got = swap(near[rows:].astype(jnp.bfloat16), "gx", 2)
    blocks = (near[:rows] + y_got.astype(jnp.float32)).reshape(rows, 4, width)
    gy_me = lax.axis_index("gy")
    token_sum = lax.dynamic_index_in_dim(blocks, gy_me, 1, keepdims=False)
    for j in range(1, 4):
        block = lax.dynamic_index_in_dim(blocks, gy_me ^ j, 1, keepdims=False)
        token_sum = token_sum + swap(block.astype(jnp.bfloat16), "gy", j).astype(jnp.float32)
    is_last = (jnp.arange(rows) == rows - 1).astype(jnp.float32)
    head_term = own_coef * reward_head.astype(jnp.float32)
    grad_tokens = lm_grad + is_last[:, None] * head_term[None, :] + token_sum
    loss_scale = 1.0 / jnp.sqrt(jnp.float32(4 * rows))

    def weight_grad(left, right):
        return jnp.einsum("tf,td->fd", left, right, preferred_element_type=jnp.float32) * loss_scale

    return (
        grad_tokens,
        weight_grad(gate_grad, tok_all),
        weight_grad(up_grad, tok_all),
        weight_grad(hidden, low_all),
        reward_tile[0, :seq_total],
    )


def body(*args):
    sizes = tuple(lax.axis_size(axis) for axis in ("gx", "gy", "gz"))
    if sizes == (4, 4, 2) and args[0].shape[0] == SEQ_LEN:
        return kernel_body(*args)
    return permute_body(*args)


def solution(mesh):
    placed = (
        P("gx", ("gz", "gy")),
        P(("gy", "gx"), "gz"),
        P(("gy", "gx"), "gz"),
        P(("gy", "gx"), "gz"),
        P(("gz", "gy")),
        P("gx", ("gz", "gy")),
        P(),
    )
    return jax.shard_map(
        body,
        mesh=mesh,
        in_specs=placed,
        out_specs=(
            P("gx", ("gz", "gy")),
            P(("gy", "gx"), "gz"),
            P(("gy", "gx"), "gz"),
            P(("gy", "gx"), "gz"),
            P(),
        ),
        check_vma=False,
    )
```

```python
import jax
import jax.numpy as jnp
from jax import lax
from jax.experimental import pallas as pl
from jax.experimental.pallas import tpu as pltpu
from jax.sharding import PartitionSpec as P

SEQ_LEN = 128


reward_weight = 64.0


def swap(value, axis, bit):
    size = lax.axis_size(axis)
    return lax.ppermute(value, axis, [(i, i ^ bit) for i in range(size)])


def bits_down(axis):
    bit = lax.axis_size(axis) // 2
    bits = []
    while bit >= 1:
        bits.append(bit)
        bit //= 2
    return bits


def gx_offsets():
    offsets = [0]
    for bit in bits_down("gx"):
        offsets = offsets + [offset ^ bit for offset in offsets]
    return offsets


def ordered_features(pieces):
    me = lax.axis_index("gy")
    stacked = jnp.stack(pieces)
    return jnp.concatenate(
        [lax.dynamic_index_in_dim(stacked, me ^ p, 0, keepdims=False) for p in range(len(pieces))],
        axis=-1,
    )


def gather_halves(shard):
    pieces = [[shard] + [swap(shard, "gy", j) for j in range(1, lax.axis_size("gy"))]]
    for bit in bits_down("gx")[:-1]:
        pieces = pieces + [[swap(piece, "gx", bit) for piece in row] for row in pieces]
    first = jnp.concatenate([ordered_features(row) for row in pieces], axis=0)
    return first, swap(first, "gx", 1)


def right_product(left, right):
    return lax.dot_general(
        left, right, (((1,), (1,)), ((), ())), preferred_element_type=jnp.float32
    )


def feature_sum(partial_value):
    size = lax.axis_size("gz")
    low = partial_value.astype(jnp.bfloat16)
    total = partial_value
    for j in range(1, size):
        total = total + swap(low, "gz", j).astype(jnp.float32)
    return total


def sum_all(value):
    for axis in ("gz", "gx", "gy"):
        for bit in bits_down(axis):
            value = value + swap(value, axis, bit)
    return value


def permute_body(tokens, gate_weight, up_weight, down_weight, reward_head, lm_grad, pair_index):
    row_count, feature_count = tokens.shape
    seq_dev = row_count // SEQ_LEN
    gx_size = lax.axis_size("gx")
    gy_size = lax.axis_size("gy")
    seq_total = seq_dev * gx_size
    me = lax.axis_index("gx")
    offsets = gx_offsets()

    tok_halves = gather_halves(tokens)
    low_halves = gather_halves(lm_grad.astype(jnp.bfloat16))
    head_own = reward_head.astype(jnp.float32)
    head_block = ordered_features(
        [reward_head] + [swap(reward_head, "gy", j) for j in range(1, gy_size)]
    )
    head_wide = jnp.broadcast_to(head_block[None, :], (8, head_block.shape[0]))
    head_part = right_product(head_wide, down_weight)[0]
    head_sum = head_part
    for j in range(1, lax.axis_size("gz")):
        head_sum = head_sum + swap(head_part, "gz", j)

    gate_halves = [feature_sum(right_product(half, gate_weight)) for half in tok_halves]
    up_halves = [feature_sum(right_product(half, up_weight)) for half in tok_halves]
    base_halves = [feature_sum(right_product(half, down_weight)) for half in low_halves]

    gate_sum = jnp.concatenate(gate_halves, axis=0)
    up_sum = jnp.concatenate(up_halves, axis=0)
    hidden_base = jnp.concatenate(base_halves, axis=0)
    tok_all = jnp.concatenate(tok_halves, axis=0)
    low_all = jnp.concatenate(low_halves, axis=0)
    unit_count = gate_sum.shape[1]

    gate_sigmoid = jax.nn.sigmoid(gate_sum)
    silu_gate = gate_sum * gate_sigmoid
    hidden = (silu_gate * up_sum).astype(jnp.bfloat16)

    last_hidden = hidden.reshape(seq_total, SEQ_LEN, unit_count)[:, SEQ_LEN - 1, :]
    last_terms = jnp.sum(last_hidden.astype(jnp.float32) * head_part[None, :], axis=1)
    last_tokens = tokens.reshape(seq_dev, SEQ_LEN, feature_count)[:, SEQ_LEN - 1, :]
    own_terms = jnp.sum(last_tokens.astype(jnp.float32) * head_own[None, :], axis=1)
    place = (me ^ jnp.array(offsets, jnp.int32))[:, None] * seq_dev + jnp.arange(seq_dev)[None, :]
    place = place.reshape(-1)
    one_hot = (place[:, None] == jnp.arange(seq_total)[None, :]).astype(jnp.float32)
    local_terms = last_terms.at[:seq_dev].add(own_terms)
    rewards = sum_all(jnp.sum(one_hot * local_terms[:, None], axis=0))

    sequence = jnp.arange(seq_total, dtype=jnp.int32)
    chosen_hot = (pair_index[:, 0:1] == sequence[None, :]).astype(jnp.float32)
    rejected_hot = (pair_index[:, 1:2] == sequence[None, :]).astype(jnp.float32)
    margin = jnp.sum(chosen_hot * rewards[None, :], axis=1) - jnp.sum(
        rejected_hot * rewards[None, :], axis=1
    )
    pair_weight = jax.nn.sigmoid(-margin)
    pair_coefs = jnp.sum((rejected_hot - chosen_hot) * pair_weight[:, None], axis=0)
    coefs = reward_weight * jnp.sum(one_hot * pair_coefs[None, :], axis=1)

    def with_last(value, vector, scales):
        count = scales.shape[0]
        is_last = (jnp.arange(SEQ_LEN) == SEQ_LEN - 1).astype(jnp.float32)
        rows = (scales[:, None] * is_last[None, :]).reshape(count * SEQ_LEN)
        return value + rows[:, None] * vector[None, :]

    hidden_grad = with_last(hidden_base, head_sum, coefs)
    up_grad = (hidden_grad * silu_gate).astype(jnp.bfloat16)
    gate_grad = (
        hidden_grad * up_sum * gate_sigmoid * (1.0 + gate_sum * (1.0 - gate_sigmoid))
    ).astype(jnp.bfloat16)

    token_part = jnp.dot(gate_grad, gate_weight, preferred_element_type=jnp.float32) + jnp.dot(
        up_grad, up_weight, preferred_element_type=jnp.float32
    )
    for bit in reversed(bits_down("gx")):
        half = token_part.shape[0] // 2
        sent = token_part[half:].astype(jnp.bfloat16)
        token_part = token_part[:half] + swap(sent, "gx", bit).astype(jnp.float32)
    blocks = token_part.reshape(row_count, gy_size, feature_count)
    gy_me = lax.axis_index("gy")
    token_sum = lax.dynamic_index_in_dim(blocks, gy_me, 1, keepdims=False)
    for j in range(1, gy_size):
        sent = lax.dynamic_index_in_dim(blocks, gy_me ^ j, 1, keepdims=False)
        token_sum = token_sum + swap(sent.astype(jnp.bfloat16), "gy", j).astype(jnp.float32)
    grad_tokens = with_last(lm_grad, head_own, coefs[:seq_dev]) + token_sum

    grad_low = with_last(
        low_all.astype(jnp.float32), head_block.astype(jnp.float32), coefs
    ).astype(jnp.bfloat16)
    loss_scale = 1.0 / jnp.sqrt(jnp.float32(row_count * gx_size))

    def weight_grad(left, right):
        return jnp.einsum("tf,td->fd", left, right, preferred_element_type=jnp.float32) * loss_scale

    return (
        grad_tokens,
        weight_grad(gate_grad, tok_all),
        weight_grad(up_grad, tok_all),
        weight_grad(hidden, grad_low),
        rewards,
    )


MESH = pl.DeviceIdType.MESH
STRIP = 16


def forward_kernel(
    tok, lm_grad, head_row, gate_hbm, up_hbm, down_hbm, diff,
    tok_out, low_out, hidden_out, gate_grad_out, up_grad_out, grad_out, reward_out,
    low, head, keep, core_sent, core_got, y_sent, y_got, z_sent, z_got,
    weight, tok_all, low_all, head_all, part, sent, got, hidden, gate_grad, up_grad,
    head_part, head_got, terms, terms_got,
    weight_sem, z_send, z_recv, head_send, head_recv, y_send, y_recv, core_send, core_recv,
    x_send, x_recv, v_send, v_recv, r_send, r_recv, out_sem,
    cs_send, cs_recv, ys_send, ys_recv, zs_send, zs_recv,
):
    rows, width = tok.shape
    units = weight.shape[1]
    me = lax.axis_index("gx")
    z = lax.axis_index("gy")
    x = lax.axis_index("gz")
    core_peer = me + 1 - 2 * lax.rem(me, 2)
    y_peer = lax.rem(me + 2, 4)
    z_from = [z, z + 1 - 2 * lax.rem(z, 2), lax.rem(z + 2, 4), 3 - z]
    chunk_owner = [me, core_peer, y_peer, 3 - me]
    x_peer = 1 - x

    def remote(src, dst, send, recv, **peer):
        return pltpu.make_async_remote_copy(
            src_ref=src, dst_ref=dst, send_sem=send, recv_sem=recv,
            device_id=peer, device_id_type=MESH,
        )

    weight_copies = [
        pltpu.make_async_copy(ref, weight.at[m], weight_sem.at[m])
        for m, ref in enumerate((gate_hbm, up_hbm, down_hbm))
    ]
    for m in (2, 0, 1):
        weight_copies[m].start()

    head[...] = jnp.broadcast_to(head_row[...].astype(jnp.float32), head.shape).astype(jnp.bfloat16)
    barrier = pltpu.get_barrier_semaphore()
    peers = [{"gy": z_from[j]} for j in (1, 2, 3)]
    peers += [{"gx": core_peer}, {"gx": y_peer}, {"gz": x_peer}]
    for peer in peers:
        pl.semaphore_signal(barrier, inc=1, device_id=peer, device_id_type=MESH)
    pl.semaphore_wait(barrier, len(peers))

    own = pl.ds(0, rows)
    other = pl.ds(rows, rows)
    pending = []

    def z_copies(a, shard, full):
        sends = [
            remote(shard, full.at[0, z, own], z_send.at[a, j - 1], z_recv.at[a, j - 1], gy=z_from[j])
            for j in (1, 2, 3)
        ]
        recvs = [
            remote(shard, full.at[0, z_from[j], own], z_send.at[a, j - 1], z_recv.at[a, j - 1],
                   gy=z_from[j])
            for j in (1, 2, 3)
        ]
        return sends, recvs

    def y_copies(a, full):
        return [
            remote(full.at[0, z_from[j], own], full.at[1, z_from[j], own],
                   y_send.at[a, j], y_recv.at[a, j], gx=y_peer)
            for j in range(4)
        ]

    def core_copies(a, full):
        return [
            remote(full.at[h, :, own], full.at[h, :, other],
                   core_send.at[a, h], core_recv.at[a, h], gx=core_peer)
            for h in range(2)
        ]

    tok_z, tok_z_recv = z_copies(0, tok, tok_all)
    low_z, low_z_recv = z_copies(1, low, low_all)
    tok_y, low_y = y_copies(0, tok_all), y_copies(1, low_all)
    tok_core, low_core = core_copies(0, tok_all), core_copies(1, low_all)

    head_z = [
        remote(head, head_all.at[z], head_send.at[j - 1], head_recv.at[j - 1], gy=z_from[j])
        for j in (1, 2, 3)
    ]
    head_z_recv = [
        remote(head, head_all.at[z_from[j]], head_send.at[j - 1], head_recv.at[j - 1], gy=z_from[j])
        for j in (1, 2, 3)
    ]
    for copy in head_z + tok_z:
        copy.start()
    tok_all[0, z, 0:rows] = tok[...]
    tok_y[0].start()
    low[...] = lm_grad[...].astype(jnp.bfloat16)
    low_all[0, z, 0:rows] = low[...]
    head_all[z] = head[...]
    part[...] = jnp.zeros_like(part)
    head_part[...] = jnp.zeros_like(head_part)

    def columns(k):
        return pl.ds(pl.multiple_of(k * width, width), width)

    def product(full, h, m):
        @pl.loop(0, 4)
        def _(k):
            part[m, h] += lax.dot_general(
                full[h, k], weight[m, :, columns(k)], (((1,), (1,)), ((), ())),
                preferred_element_type=jnp.float32,
            )

        sent[m, h] = part[m, h].astype(jnp.bfloat16)
        x_copies[m][h].start()

    x_copies = [
        [
            remote(sent.at[m, h], got.at[m, h], x_send.at[m, h], x_recv.at[m, h], gz=x_peer)
            for h in range(2)
        ]
        for m in range(3)
    ]

    for copy in head_z_recv:
        copy.wait_recv()
    weight_copies[2].wait()

    @pl.loop(0, 4)
    def _(k):
        head_part[...] += lax.dot_general(
            head_all[k], weight[2, :, columns(k)], (((1,), (1,)), ((), ())),
            preferred_element_type=jnp.float32,
        )

    head_copy = remote(head_part, head_got, v_send, v_recv, gz=x_peer)
    head_copy.start()

    for j in (1, 2, 3):
        tok_z_recv[j - 1].wait_recv()
        tok_y[j].start()
    tok_core[0].start()
    for copy in low_z:
        copy.start()
    weight_copies[0].wait()
    tok_core[0].wait_recv()
    product(tok_all, 0, 0)
    weight_copies[1].wait()
    product(tok_all, 0, 1)

    for copy in tok_y:
        copy.wait_recv()
    tok_core[1].start()
    low_y[0].start()
    tok_core[1].wait_recv()
    tok_stores = [
        pltpu.make_async_copy(
            tok_all.at[:, k], tok_out.at[:, :, pl.ds(k * width, width)], out_sem.at[k]
        )
        for k in range(4)
    ]
    for copy in tok_stores:
        copy.start()
    product(tok_all, 1, 0)
    for j in (1, 2, 3):
        low_z_recv[j - 1].wait_recv()
        low_y[j].start()
    low_core[0].start()
    product(tok_all, 1, 1)
    low_core[0].wait_recv()
    product(low_all, 0, 2)

    def activate(h):
        x_copies[0][h].wait_recv()
        x_copies[1][h].wait_recv()

        @pl.loop(0, 2 * rows // STRIP)
        def _(i):
            strip = pl.ds(pl.multiple_of(i * STRIP, STRIP), STRIP)
            gate_sum = part[0, h, strip] + got[0, h, strip].astype(jnp.float32)
            up_sum = part[1, h, strip] + got[1, h, strip].astype(jnp.float32)
            gate_sigmoid = jax.nn.sigmoid(gate_sum)
            silu_gate = gate_sum * gate_sigmoid
            hidden[h, strip] = (silu_gate * up_sum).astype(jnp.bfloat16)
            part[0, h, strip] = silu_gate
            part[1, h, strip] = up_sum * gate_sigmoid * (1.0 + gate_sum * (1.0 - gate_sigmoid))

    activate(0)
    for copy in low_y:
        copy.wait_recv()
    low_core[1].start()
    low_core[1].wait_recv()
    product(low_all, 1, 2)
    activate(1)
    hidden_store = pltpu.make_async_copy(hidden, hidden_out, out_sem.at[4])
    hidden_store.start()

    lane = lax.broadcasted_iota(jnp.int32, (8, 128), 1)
    last = pl.ds(rows - STRIP, STRIP)
    own_term = jnp.sum(
        tok[last].astype(jnp.float32)[STRIP - 1:] * head[...].astype(jnp.float32)[0:1],
        axis=1, keepdims=True,
    )
    tile = jnp.zeros((8, 128), jnp.float32)
    for c in range(4):
        rows_c = pl.ds((c % 2) * rows + rows - STRIP, STRIP)
        term = jnp.sum(
            hidden[c // 2, rows_c].astype(jnp.float32)[STRIP - 1:] * head_part[0:1],
            axis=1, keepdims=True,
        )
        if c == 0:
            term = term + own_term
        tile = tile + jnp.where(lane == chunk_owner[c], jnp.broadcast_to(term, (8, 128)), 0.0)
    steps = [{"gz": x_peer}, {"gx": core_peer}, {"gx": y_peer}, {"gy": z_from[1]}, {"gy": z_from[2]}]
    for k, peer in enumerate(steps):
        terms[k] = tile
        copy = remote(terms.at[k], terms_got.at[k], r_send.at[k], r_recv.at[k], **peer)
        copy.start()
        copy.wait_recv()
        pending.append(copy)
        tile = tile + terms_got[k]
    reward_out[...] = tile
    pair_weight = jax.nn.sigmoid(jnp.sum(diff[...] * tile, axis=1, keepdims=True))
    coefs = reward_weight * jnp.sum(diff[...] * pair_weight, axis=0, keepdims=True)
    coefs = jnp.broadcast_to(coefs, (8, 128))
    chunk_coef = [
        jnp.sum(jnp.where(lane == chunk_owner[c], coefs, 0.0), axis=1, keepdims=True)[0:1]
        for c in range(4)
    ]

    row = lax.broadcasted_iota(jnp.int32, (STRIP, 1), 0)

    for copy in low_y + low_core:
        copy.wait_send()
    for c in range(4):
        rows_c = pl.ds((c % 2) * rows + rows - STRIP, STRIP)
        scale = jnp.where(row == STRIP - 1, chunk_coef[c], 0.0)
        for k in range(4):
            value = low_all[c // 2, k, rows_c].astype(jnp.float32)
            value = value + scale * head_all[k].astype(jnp.float32)
            low_all[c // 2, k, rows_c] = value.astype(jnp.bfloat16)
    low_stores = [
        pltpu.make_async_copy(
            low_all.at[:, k], low_out.at[:, :, pl.ds(k * width, width)], out_sem.at[5 + k]
        )
        for k in range(4)
    ]
    for copy in low_stores:
        copy.start()

    head_copy.wait_recv()
    head_sum = head_part[0:1] + head_got[0:1]

    def core_sum(h, j):
        return remote(core_sent.at[h, z_from[j]], core_got.at[h, z_from[j]],
                      cs_send.at[h, j], cs_recv.at[h, j], gx=core_peer)

    def y_sum(j):
        return remote(y_sent.at[z_from[j]], y_got.at[z_from[j]], ys_send.at[j], ys_recv.at[j], gx=y_peer)

    def z_sum(j):
        return remote(z_sent.at[j - 1], z_got.at[j - 1], zs_send.at[j - 1], zs_recv.at[j - 1],
                      gy=z_from[j])

    def send_y(j):
        core_sum(1, j).wait_recv()
        k = z_from[j]
        y_sent[k] = (keep[1, k] + core_got[1, k].astype(jnp.float32)).astype(jnp.bfloat16)
        y_sum(j).start()

    order = (3, 2, 1, 0)
    for h in range(2):
        x_copies[2][h].wait_recv()
        for b in range(2):
            coef = chunk_coef[2 * h + b]

            @pl.loop(b * rows // STRIP, (b + 1) * rows // STRIP)
            def _(i):
                strip = pl.ds(pl.multiple_of(i * STRIP, STRIP), STRIP)
                at = row + (i * STRIP - b * rows)
                scale = jnp.where(at == rows - 1, coef, 0.0)
                grad = part[2, h, strip] + got[2, h, strip].astype(jnp.float32)
                grad = grad + scale * head_sum
                up_grad[h, strip] = (grad * part[0, h, strip]).astype(jnp.bfloat16)
                gate_grad[h, strip] = (grad * part[1, h, strip]).astype(jnp.bfloat16)

        for n, j in enumerate(order):
            k = z_from[j]
            value = jnp.dot(
                gate_grad[h], weight[0, :, columns(k)], preferred_element_type=jnp.float32
            ) + jnp.dot(up_grad[h], weight[1, :, columns(k)], preferred_element_type=jnp.float32)
            core_sent[h, k] = value[rows:].astype(jnp.bfloat16)
            core_sum(h, j).start()
            keep[h, k] = value[:rows]
            if h == 1 and n > 0:
                send_y(order[n - 1])
    send_y(order[-1])

    stores = [
        pltpu.make_async_copy(gate_grad, gate_grad_out, out_sem.at[9]),
        pltpu.make_async_copy(up_grad, up_grad_out, out_sem.at[10]),
    ]
    for copy in stores:
        copy.start()
    for j in order:
        k = z_from[j]
        core_sum(0, j).wait_recv()
        near = keep[0, k] + core_got[0, k].astype(jnp.float32)
        y_sum(j).wait_recv()
        near = near + y_got[k].astype(jnp.float32)
        if j > 0:
            z_sent[j - 1] = near.astype(jnp.bfloat16)
            z_sum(j).start()
        else:
            grad_out[...] = lm_grad[...] + near
    for j in (3, 2, 1):
        z_sum(j).wait_recv()
        grad_out[...] += z_got[j - 1].astype(jnp.float32)
    scale = jnp.where(row == STRIP - 1, chunk_coef[0], 0.0)
    grad_out[last] += scale * head[...].astype(jnp.float32)

    for j in order:
        core_sum(0, j).wait_send()
        core_sum(1, j).wait_send()
        y_sum(j).wait_send()
        if j > 0:
            z_sum(j).wait_send()
    for copy in head_z + tok_z + low_z + tok_y + tok_core + [head_copy] + pending:
        copy.wait_send()
    for copies in x_copies:
        for copy in copies:
            copy.wait_send()
    for copy in tok_stores + low_stores + stores + [hidden_store]:
        copy.wait()


def forward_call(tokens, lm_grad, head_row, gate_weight, up_weight, down_weight, diff):
    rows, width = tokens.shape
    units, features = gate_weight.shape
    low_type, f32 = jnp.bfloat16, jnp.float32
    struct = jax.ShapeDtypeStruct
    vmem = pl.BlockSpec(memory_space=pltpu.VMEM)
    hbm = pl.BlockSpec(memory_space=pl.ANY)
    dma = pltpu.SemaphoreType.DMA
    flops = 6 * 4 * rows * units * features
    return pl.pallas_call(
        forward_kernel,
        out_shape=[
            struct((2, 2 * rows, features), low_type),
            struct((2, 2 * rows, features), low_type),
            struct((2, 2 * rows, units), low_type),
            struct((2, 2 * rows, units), low_type),
            struct((2, 2 * rows, units), low_type),
            struct((rows, width), f32),
            struct((8, 128), f32),
        ],
        in_specs=[vmem, vmem, vmem, hbm, hbm, hbm, vmem],
        out_specs=[hbm, hbm, hbm, hbm, hbm, vmem, vmem],
        scratch_shapes=[
            pltpu.VMEM((rows, width), low_type),
            pltpu.VMEM((16, width), low_type),
            pltpu.VMEM((2, 4, rows, width), f32),
            pltpu.VMEM((2, 4, rows, width), low_type),
            pltpu.VMEM((2, 4, rows, width), low_type),
            pltpu.VMEM((4, rows, width), low_type),
            pltpu.VMEM((4, rows, width), low_type),
            pltpu.VMEM((3, rows, width), low_type),
            pltpu.VMEM((3, rows, width), low_type),
            pltpu.VMEM((3, units, features), low_type),
            pltpu.VMEM((2, 4, 2 * rows, width), low_type),
            pltpu.VMEM((2, 4, 2 * rows, width), low_type),
            pltpu.VMEM((4, 16, width), low_type),
            pltpu.VMEM((3, 2, 2 * rows, units), f32),
            pltpu.VMEM((3, 2, 2 * rows, units), low_type),
            pltpu.VMEM((3, 2, 2 * rows, units), low_type),
            pltpu.VMEM((2, 2 * rows, units), low_type),
            pltpu.VMEM((2, 2 * rows, units), low_type),
            pltpu.VMEM((2, 2 * rows, units), low_type),
            pltpu.VMEM((16, units), f32),
            pltpu.VMEM((16, units), f32),
            pltpu.VMEM((5, 8, 128), f32),
            pltpu.VMEM((5, 8, 128), f32),
            dma((3,)), dma((2, 3)), dma((2, 3)), dma((3,)), dma((3,)),
            dma((2, 4)), dma((2, 4)), dma((2, 2)), dma((2, 2)),
            dma((3, 2)), dma((3, 2)), dma(()), dma(()), dma((5,)), dma((5,)), dma((11,)),
            dma((2, 4)), dma((2, 4)), dma((4,)), dma((4,)), dma((3,)), dma((3,)),
        ],
        compiler_params=pltpu.CompilerParams(
            collective_id=0, has_side_effects=True, vmem_limit_bytes=62 * 1024 * 1024
        ),
        cost_estimate=pl.CostEstimate(
            flops=flops, bytes_accessed=3 * units * features * 2, transcendentals=0
        ),
    )(tokens, lm_grad, head_row, gate_weight, up_weight, down_weight, diff)


def kernel_body(tokens, gate_weight, up_weight, down_weight, reward_head, lm_grad, pair_index):
    rows, width = tokens.shape
    units, features = gate_weight.shape
    seq_total = lax.axis_size("gx")
    sequence = jnp.arange(128, dtype=jnp.int32)
    diff = (pair_index[:, 1:2] == sequence[None, :]).astype(jnp.float32) - (
        pair_index[:, 0:1] == sequence[None, :]
    ).astype(jnp.float32)
    diff = jnp.pad(diff, ((0, 8 - diff.shape[0]), (0, 0)))
    tok_all, low_all, hidden, gate_grad, up_grad, grad_tokens, reward_tile = forward_call(
        tokens, lm_grad, reward_head[None, :], gate_weight, up_weight, down_weight, diff
    )
    tok_all = tok_all.reshape(4 * rows, features)
    low_all = low_all.reshape(4 * rows, features)
    hidden = hidden.reshape(4 * rows, units)
    gate_grad = gate_grad.reshape(4 * rows, units)
    up_grad = up_grad.reshape(4 * rows, units)
    loss_scale = 1.0 / jnp.sqrt(jnp.float32(4 * rows))

    def weight_grad(left, right):
        return jnp.einsum("tf,td->fd", left, right, preferred_element_type=jnp.float32) * loss_scale

    return (
        grad_tokens,
        weight_grad(gate_grad, tok_all),
        weight_grad(up_grad, tok_all),
        weight_grad(hidden, low_all),
        reward_tile[0, :seq_total],
    )


def body(*args):
    sizes = tuple(lax.axis_size(axis) for axis in ("gx", "gy", "gz"))
    if sizes == (4, 4, 2) and args[0].shape[0] == SEQ_LEN:
        return kernel_body(*args)
    return permute_body(*args)


def solution(mesh):
    placed = (
        P("gx", ("gz", "gy")),
        P(("gy", "gx"), "gz"),
        P(("gy", "gx"), "gz"),
        P(("gy", "gx"), "gz"),
        P(("gz", "gy")),
        P("gx", ("gz", "gy")),
        P(),
    )
    return jax.shard_map(
        body,
        mesh=mesh,
        in_specs=placed,
        out_specs=(
            P("gx", ("gz", "gy")),
            P(("gy", "gx"), "gz"),
            P(("gy", "gx"), "gz"),
            P(("gy", "gx"), "gz"),
            P(),
        ),
        check_vma=False,
    )
```

```python
import jax
import jax.numpy as jnp
from jax import lax
from jax.experimental import pallas as pl
from jax.experimental.pallas import tpu as pltpu
from jax.sharding import PartitionSpec as P

SEQ_LEN = 128


reward_weight = 64.0


def swap(value, axis, bit):
    size = lax.axis_size(axis)
    return lax.ppermute(value, axis, [(i, i ^ bit) for i in range(size)])


def bits_down(axis):
    bit = lax.axis_size(axis) // 2
    bits = []
    while bit >= 1:
        bits.append(bit)
        bit //= 2
    return bits


def gx_offsets():
    offsets = [0]
    for bit in bits_down("gx"):
        offsets = offsets + [offset ^ bit for offset in offsets]
    return offsets


def ordered_features(pieces):
    me = lax.axis_index("gy")
    stacked = jnp.stack(pieces)
    return jnp.concatenate(
        [lax.dynamic_index_in_dim(stacked, me ^ p, 0, keepdims=False) for p in range(len(pieces))],
        axis=-1,
    )


def gather_halves(shard):
    pieces = [[shard] + [swap(shard, "gy", j) for j in range(1, lax.axis_size("gy"))]]
    for bit in bits_down("gx")[:-1]:
        pieces = pieces + [[swap(piece, "gx", bit) for piece in row] for row in pieces]
    first = jnp.concatenate([ordered_features(row) for row in pieces], axis=0)
    return first, swap(first, "gx", 1)


def right_product(left, right):
    return lax.dot_general(
        left, right, (((1,), (1,)), ((), ())), preferred_element_type=jnp.float32
    )


def feature_sum(partial_value):
    size = lax.axis_size("gz")
    low = partial_value.astype(jnp.bfloat16)
    total = partial_value
    for j in range(1, size):
        total = total + swap(low, "gz", j).astype(jnp.float32)
    return total


def sum_all(value):
    for axis in ("gz", "gx", "gy"):
        for bit in bits_down(axis):
            value = value + swap(value, axis, bit)
    return value


def permute_body(tokens, gate_weight, up_weight, down_weight, reward_head, lm_grad, pair_index):
    row_count, feature_count = tokens.shape
    seq_dev = row_count // SEQ_LEN
    gx_size = lax.axis_size("gx")
    gy_size = lax.axis_size("gy")
    seq_total = seq_dev * gx_size
    me = lax.axis_index("gx")
    offsets = gx_offsets()

    tok_halves = gather_halves(tokens)
    low_halves = gather_halves(lm_grad.astype(jnp.bfloat16))
    head_own = reward_head.astype(jnp.float32)
    head_block = ordered_features(
        [reward_head] + [swap(reward_head, "gy", j) for j in range(1, gy_size)]
    )
    head_wide = jnp.broadcast_to(head_block[None, :], (8, head_block.shape[0]))
    head_part = right_product(head_wide, down_weight)[0]
    head_sum = head_part
    for j in range(1, lax.axis_size("gz")):
        head_sum = head_sum + swap(head_part, "gz", j)

    gate_halves = [feature_sum(right_product(half, gate_weight)) for half in tok_halves]
    up_halves = [feature_sum(right_product(half, up_weight)) for half in tok_halves]
    base_halves = [feature_sum(right_product(half, down_weight)) for half in low_halves]

    gate_sum = jnp.concatenate(gate_halves, axis=0)
    up_sum = jnp.concatenate(up_halves, axis=0)
    hidden_base = jnp.concatenate(base_halves, axis=0)
    tok_all = jnp.concatenate(tok_halves, axis=0)
    low_all = jnp.concatenate(low_halves, axis=0)
    unit_count = gate_sum.shape[1]

    gate_sigmoid = jax.nn.sigmoid(gate_sum)
    silu_gate = gate_sum * gate_sigmoid
    hidden = (silu_gate * up_sum).astype(jnp.bfloat16)

    last_hidden = hidden.reshape(seq_total, SEQ_LEN, unit_count)[:, SEQ_LEN - 1, :]
    last_terms = jnp.sum(last_hidden.astype(jnp.float32) * head_part[None, :], axis=1)
    last_tokens = tokens.reshape(seq_dev, SEQ_LEN, feature_count)[:, SEQ_LEN - 1, :]
    own_terms = jnp.sum(last_tokens.astype(jnp.float32) * head_own[None, :], axis=1)
    place = (me ^ jnp.array(offsets, jnp.int32))[:, None] * seq_dev + jnp.arange(seq_dev)[None, :]
    place = place.reshape(-1)
    one_hot = (place[:, None] == jnp.arange(seq_total)[None, :]).astype(jnp.float32)
    local_terms = last_terms.at[:seq_dev].add(own_terms)
    rewards = sum_all(jnp.sum(one_hot * local_terms[:, None], axis=0))

    sequence = jnp.arange(seq_total, dtype=jnp.int32)
    chosen_hot = (pair_index[:, 0:1] == sequence[None, :]).astype(jnp.float32)
    rejected_hot = (pair_index[:, 1:2] == sequence[None, :]).astype(jnp.float32)
    margin = jnp.sum(chosen_hot * rewards[None, :], axis=1) - jnp.sum(
        rejected_hot * rewards[None, :], axis=1
    )
    pair_weight = jax.nn.sigmoid(-margin)
    pair_coefs = jnp.sum((rejected_hot - chosen_hot) * pair_weight[:, None], axis=0)
    coefs = reward_weight * jnp.sum(one_hot * pair_coefs[None, :], axis=1)

    def with_last(value, vector, scales):
        count = scales.shape[0]
        is_last = (jnp.arange(SEQ_LEN) == SEQ_LEN - 1).astype(jnp.float32)
        rows = (scales[:, None] * is_last[None, :]).reshape(count * SEQ_LEN)
        return value + rows[:, None] * vector[None, :]

    hidden_grad = with_last(hidden_base, head_sum, coefs)
    up_grad = (hidden_grad * silu_gate).astype(jnp.bfloat16)
    gate_grad = (
        hidden_grad * up_sum * gate_sigmoid * (1.0 + gate_sum * (1.0 - gate_sigmoid))
    ).astype(jnp.bfloat16)

    token_part = jnp.dot(gate_grad, gate_weight, preferred_element_type=jnp.float32) + jnp.dot(
        up_grad, up_weight, preferred_element_type=jnp.float32
    )
    for bit in reversed(bits_down("gx")):
        half = token_part.shape[0] // 2
        sent = token_part[half:].astype(jnp.bfloat16)
        token_part = token_part[:half] + swap(sent, "gx", bit).astype(jnp.float32)
    blocks = token_part.reshape(row_count, gy_size, feature_count)
    gy_me = lax.axis_index("gy")
    token_sum = lax.dynamic_index_in_dim(blocks, gy_me, 1, keepdims=False)
    for j in range(1, gy_size):
        sent = lax.dynamic_index_in_dim(blocks, gy_me ^ j, 1, keepdims=False)
        token_sum = token_sum + swap(sent.astype(jnp.bfloat16), "gy", j).astype(jnp.float32)
    grad_tokens = with_last(lm_grad, head_own, coefs[:seq_dev]) + token_sum

    grad_low = with_last(
        low_all.astype(jnp.float32), head_block.astype(jnp.float32), coefs
    ).astype(jnp.bfloat16)
    loss_scale = 1.0 / jnp.sqrt(jnp.float32(row_count * gx_size))

    def weight_grad(left, right):
        return jnp.einsum("tf,td->fd", left, right, preferred_element_type=jnp.float32) * loss_scale

    return (
        grad_tokens,
        weight_grad(gate_grad, tok_all),
        weight_grad(up_grad, tok_all),
        weight_grad(hidden, grad_low),
        rewards,
    )


MESH = pl.DeviceIdType.MESH
STRIP = 16


def forward_kernel(
    tok, lm_grad, head_row, gate_hbm, up_hbm, down_hbm, diff,
    tok_out, low_out, hidden_out, gate_grad_out, up_grad_out, grad_out, reward_out,
    low, head, keep, core_sent, core_got, y_sent, y_got, z_sent, z_got,
    weight, tok_all, low_all, head_all, part, sent, got, hidden, gate_grad, up_grad,
    head_part, head_got, terms, terms_got,
    weight_sem, z_send, z_recv, head_send, head_recv, y_send, y_recv, core_send, core_recv,
    x_send, x_recv, v_send, v_recv, r_send, r_recv, out_sem,
    cs_send, cs_recv, ys_send, ys_recv, zs_send, zs_recv,
):
    rows, width = tok.shape
    units = weight.shape[1]
    me = lax.axis_index("gx")
    z = lax.axis_index("gy")
    x = lax.axis_index("gz")
    core_peer = me + 1 - 2 * lax.rem(me, 2)
    y_peer = lax.rem(me + 2, 4)
    z_from = [z, z + 1 - 2 * lax.rem(z, 2), lax.rem(z + 2, 4), 3 - z]
    chunk_owner = [me, core_peer, y_peer, 3 - me]
    x_peer = 1 - x

    def remote(src, dst, send, recv, **peer):
        return pltpu.make_async_remote_copy(
            src_ref=src, dst_ref=dst, send_sem=send, recv_sem=recv,
            device_id=peer, device_id_type=MESH,
        )

    weight_copies = [
        pltpu.make_async_copy(ref, weight.at[m], weight_sem.at[m])
        for m, ref in enumerate((gate_hbm, up_hbm, down_hbm))
    ]
    for m in (2, 0, 1):
        weight_copies[m].start()

    head[...] = jnp.broadcast_to(head_row[...].astype(jnp.float32), head.shape).astype(jnp.bfloat16)
    barrier = pltpu.get_barrier_semaphore()
    peers = [{"gy": z_from[j]} for j in (1, 2, 3)]
    peers += [{"gx": core_peer}, {"gx": y_peer}, {"gz": x_peer}]
    for peer in peers:
        pl.semaphore_signal(barrier, inc=1, device_id=peer, device_id_type=MESH)
    pl.semaphore_wait(barrier, len(peers))

    own = pl.ds(0, rows)
    other = pl.ds(rows, rows)
    pending = []

    def z_copies(a, shard, full):
        sends = [
            remote(shard, full.at[0, z, own], z_send.at[a, j - 1], z_recv.at[a, j - 1], gy=z_from[j])
            for j in (1, 2, 3)
        ]
        recvs = [
            remote(shard, full.at[0, z_from[j], own], z_send.at[a, j - 1], z_recv.at[a, j - 1],
                   gy=z_from[j])
            for j in (1, 2, 3)
        ]
        return sends, recvs

    def y_copies(a, full):
        return [
            remote(full.at[0, z_from[j], own], full.at[1, z_from[j], own],
                   y_send.at[a, j], y_recv.at[a, j], gx=y_peer)
            for j in range(4)
        ]

    def core_copies(a, full):
        return [
            remote(full.at[h, :, own], full.at[h, :, other],
                   core_send.at[a, h], core_recv.at[a, h], gx=core_peer)
            for h in range(2)
        ]

    tok_z, tok_z_recv = z_copies(0, tok, tok_all)
    low_z, low_z_recv = z_copies(1, low, low_all)
    tok_y, low_y = y_copies(0, tok_all), y_copies(1, low_all)
    tok_core, low_core = core_copies(0, tok_all), core_copies(1, low_all)

    head_z = [
        remote(head, head_all.at[z], head_send.at[j - 1], head_recv.at[j - 1], gy=z_from[j])
        for j in (1, 2, 3)
    ]
    head_z_recv = [
        remote(head, head_all.at[z_from[j]], head_send.at[j - 1], head_recv.at[j - 1], gy=z_from[j])
        for j in (1, 2, 3)
    ]
    for copy in head_z + tok_z:
        copy.start()
    tok_all[0, z, 0:rows] = tok[...]
    tok_y[0].start()
    low[...] = lm_grad[...].astype(jnp.bfloat16)
    low_all[0, z, 0:rows] = low[...]
    head_all[z] = head[...]
    part[...] = jnp.zeros_like(part)
    head_part[...] = jnp.zeros_like(head_part)

    def columns(k):
        return pl.ds(pl.multiple_of(k * width, width), width)

    def product(full, h, m):
        for n, block in enumerate(unit_blocks):

            @pl.loop(0, 4)
            def _(k):
                part[m, h, :, block] += lax.dot_general(
                    full[h, k], weight[m, block, columns(k)], (((1,), (1,)), ((), ())),
                    preferred_element_type=jnp.float32,
                )

            sent[m, h, :, block] = part[m, h, :, block].astype(jnp.bfloat16)
            x_copies[m][h][n].start()

    first_units = -(-units // 512) * 256
    unit_blocks = [pl.ds(0, first_units), pl.ds(first_units, units - first_units)]
    x_copies = [
        [
            [
                remote(sent.at[m, h, :, block], got.at[m, h, :, block],
                       x_send.at[m, h, n], x_recv.at[m, h, n], gz=x_peer)
                for n, block in enumerate(unit_blocks)
            ]
            for h in range(2)
        ]
        for m in range(3)
    ]

    for copy in head_z_recv:
        copy.wait_recv()
    weight_copies[2].wait()

    @pl.loop(0, 4)
    def _(k):
        head_part[...] += lax.dot_general(
            head_all[k], weight[2, :, columns(k)], (((1,), (1,)), ((), ())),
            preferred_element_type=jnp.float32,
        )

    head_copy = remote(head_part, head_got, v_send, v_recv, gz=x_peer)
    head_copy.start()

    for j in (1, 2, 3):
        tok_z_recv[j - 1].wait_recv()
        tok_y[j].start()
    tok_core[0].start()
    for copy in low_z:
        copy.start()
    weight_copies[0].wait()
    tok_core[0].wait_recv()
    product(tok_all, 0, 0)
    weight_copies[1].wait()
    product(tok_all, 0, 1)

    for copy in tok_y:
        copy.wait_recv()
    tok_core[1].start()
    low_y[0].start()
    tok_core[1].wait_recv()
    tok_stores = [
        pltpu.make_async_copy(
            tok_all.at[:, k], tok_out.at[:, :, pl.ds(k * width, width)], out_sem.at[k]
        )
        for k in range(4)
    ]
    for copy in tok_stores:
        copy.start()
    product(tok_all, 1, 0)
    for j in (1, 2, 3):
        low_z_recv[j - 1].wait_recv()
        low_y[j].start()
    low_core[0].start()
    product(tok_all, 1, 1)
    low_core[0].wait_recv()
    product(low_all, 0, 2)

    def activate(h):
        for copy in x_copies[0][h] + x_copies[1][h]:
            copy.wait_recv()

        @pl.loop(0, 2 * rows // STRIP)
        def _(i):
            strip = pl.ds(pl.multiple_of(i * STRIP, STRIP), STRIP)
            gate_sum = part[0, h, strip] + got[0, h, strip].astype(jnp.float32)
            up_sum = part[1, h, strip] + got[1, h, strip].astype(jnp.float32)
            gate_sigmoid = jax.nn.sigmoid(gate_sum)
            silu_gate = gate_sum * gate_sigmoid
            hidden[h, strip] = (silu_gate * up_sum).astype(jnp.bfloat16)
            part[0, h, strip] = silu_gate
            part[1, h, strip] = up_sum * gate_sigmoid * (1.0 + gate_sum * (1.0 - gate_sigmoid))

    activate(0)
    for copy in low_y:
        copy.wait_recv()
    low_core[1].start()
    low_core[1].wait_recv()
    product(low_all, 1, 2)
    activate(1)
    hidden_store = pltpu.make_async_copy(hidden, hidden_out, out_sem.at[4])
    hidden_store.start()

    lane = lax.broadcasted_iota(jnp.int32, (8, 128), 1)
    last = pl.ds(rows - STRIP, STRIP)
    own_term = jnp.sum(
        tok[last].astype(jnp.float32)[STRIP - 1:] * head[...].astype(jnp.float32)[0:1],
        axis=1, keepdims=True,
    )
    tile = jnp.zeros((8, 128), jnp.float32)
    for c in range(4):
        rows_c = pl.ds((c % 2) * rows + rows - STRIP, STRIP)
        term = jnp.sum(
            hidden[c // 2, rows_c].astype(jnp.float32)[STRIP - 1:] * head_part[0:1],
            axis=1, keepdims=True,
        )
        if c == 0:
            term = term + own_term
        tile = tile + jnp.where(lane == chunk_owner[c], jnp.broadcast_to(term, (8, 128)), 0.0)
    steps = [{"gz": x_peer}, {"gx": core_peer}, {"gx": y_peer}, {"gy": z_from[1]}, {"gy": z_from[2]}]
    for k, peer in enumerate(steps):
        terms[k] = tile
        copy = remote(terms.at[k], terms_got.at[k], r_send.at[k], r_recv.at[k], **peer)
        copy.start()
        copy.wait_recv()
        pending.append(copy)
        tile = tile + terms_got[k]
    reward_out[...] = tile
    pair_weight = jax.nn.sigmoid(jnp.sum(diff[...] * tile, axis=1, keepdims=True))
    coefs = reward_weight * jnp.sum(diff[...] * pair_weight, axis=0, keepdims=True)
    coefs = jnp.broadcast_to(coefs, (8, 128))
    chunk_coef = [
        jnp.sum(jnp.where(lane == chunk_owner[c], coefs, 0.0), axis=1, keepdims=True)[0:1]
        for c in range(4)
    ]

    row = lax.broadcasted_iota(jnp.int32, (STRIP, 1), 0)

    for copy in low_y + low_core:
        copy.wait_send()
    for c in range(4):
        rows_c = pl.ds((c % 2) * rows + rows - STRIP, STRIP)
        scale = jnp.where(row == STRIP - 1, chunk_coef[c], 0.0)
        for k in range(4):
            value = low_all[c // 2, k, rows_c].astype(jnp.float32)
            value = value + scale * head_all[k].astype(jnp.float32)
            low_all[c // 2, k, rows_c] = value.astype(jnp.bfloat16)
    low_stores = [
        pltpu.make_async_copy(
            low_all.at[:, k], low_out.at[:, :, pl.ds(k * width, width)], out_sem.at[5 + k]
        )
        for k in range(4)
    ]
    for copy in low_stores:
        copy.start()

    head_copy.wait_recv()
    head_sum = head_part[0:1] + head_got[0:1]

    def core_sum(h, j):
        return remote(core_sent.at[h, z_from[j]], core_got.at[h, z_from[j]],
                      cs_send.at[h, j], cs_recv.at[h, j], gx=core_peer)

    def y_sum(j):
        return remote(y_sent.at[z_from[j]], y_got.at[z_from[j]], ys_send.at[j], ys_recv.at[j], gx=y_peer)

    def z_sum(j):
        return remote(z_sent.at[j - 1], z_got.at[j - 1], zs_send.at[j - 1], zs_recv.at[j - 1],
                      gy=z_from[j])

    def send_y(j):
        core_sum(1, j).wait_recv()
        k = z_from[j]
        y_sent[k] = (keep[1, k] + core_got[1, k].astype(jnp.float32)).astype(jnp.bfloat16)
        y_sum(j).start()

    order = (3, 2, 1, 0)
    for h in range(2):
        for copy in x_copies[2][h]:
            copy.wait_recv()
        for b in range(2):
            coef = chunk_coef[2 * h + b]

            @pl.loop(b * rows // STRIP, (b + 1) * rows // STRIP)
            def _(i):
                strip = pl.ds(pl.multiple_of(i * STRIP, STRIP), STRIP)
                at = row + (i * STRIP - b * rows)
                scale = jnp.where(at == rows - 1, coef, 0.0)
                grad = part[2, h, strip] + got[2, h, strip].astype(jnp.float32)
                grad = grad + scale * head_sum
                up_grad[h, strip] = (grad * part[0, h, strip]).astype(jnp.bfloat16)
                gate_grad[h, strip] = (grad * part[1, h, strip]).astype(jnp.bfloat16)

        for n, j in enumerate(order):
            k = z_from[j]
            value = jnp.dot(
                gate_grad[h], weight[0, :, columns(k)], preferred_element_type=jnp.float32
            ) + jnp.dot(up_grad[h], weight[1, :, columns(k)], preferred_element_type=jnp.float32)
            core_sent[h, k] = value[rows:].astype(jnp.bfloat16)
            core_sum(h, j).start()
            keep[h, k] = value[:rows]
            if h == 1 and n > 0:
                send_y(order[n - 1])
    send_y(order[-1])

    stores = [
        pltpu.make_async_copy(gate_grad, gate_grad_out, out_sem.at[9]),
        pltpu.make_async_copy(up_grad, up_grad_out, out_sem.at[10]),
    ]
    for copy in stores:
        copy.start()
    for j in order:
        k = z_from[j]
        core_sum(0, j).wait_recv()
        near = keep[0, k] + core_got[0, k].astype(jnp.float32)
        y_sum(j).wait_recv()
        near = near + y_got[k].astype(jnp.float32)
        if j > 0:
            z_sent[j - 1] = near.astype(jnp.bfloat16)
            z_sum(j).start()
        else:
            grad_out[...] = lm_grad[...] + near
    for j in (3, 2, 1):
        z_sum(j).wait_recv()
        grad_out[...] += z_got[j - 1].astype(jnp.float32)
    scale = jnp.where(row == STRIP - 1, chunk_coef[0], 0.0)
    grad_out[last] += scale * head[...].astype(jnp.float32)

    for j in order:
        core_sum(0, j).wait_send()
        core_sum(1, j).wait_send()
        y_sum(j).wait_send()
        if j > 0:
            z_sum(j).wait_send()
    for copy in head_z + tok_z + low_z + tok_y + tok_core + [head_copy] + pending:
        copy.wait_send()
    for copies in x_copies:
        for copy in copies[0] + copies[1]:
            copy.wait_send()
    for copy in tok_stores + low_stores + stores + [hidden_store]:
        copy.wait()


def forward_call(tokens, lm_grad, head_row, gate_weight, up_weight, down_weight, diff):
    rows, width = tokens.shape
    units, features = gate_weight.shape
    low_type, f32 = jnp.bfloat16, jnp.float32
    struct = jax.ShapeDtypeStruct
    vmem = pl.BlockSpec(memory_space=pltpu.VMEM)
    hbm = pl.BlockSpec(memory_space=pl.ANY)
    dma = pltpu.SemaphoreType.DMA
    flops = 6 * 4 * rows * units * features
    return pl.pallas_call(
        forward_kernel,
        out_shape=[
            struct((2, 2 * rows, features), low_type),
            struct((2, 2 * rows, features), low_type),
            struct((2, 2 * rows, units), low_type),
            struct((2, 2 * rows, units), low_type),
            struct((2, 2 * rows, units), low_type),
            struct((rows, width), f32),
            struct((8, 128), f32),
        ],
        in_specs=[vmem, vmem, vmem, hbm, hbm, hbm, vmem],
        out_specs=[hbm, hbm, hbm, hbm, hbm, vmem, vmem],
        scratch_shapes=[
            pltpu.VMEM((rows, width), low_type),
            pltpu.VMEM((16, width), low_type),
            pltpu.VMEM((2, 4, rows, width), f32),
            pltpu.VMEM((2, 4, rows, width), low_type),
            pltpu.VMEM((2, 4, rows, width), low_type),
            pltpu.VMEM((4, rows, width), low_type),
            pltpu.VMEM((4, rows, width), low_type),
            pltpu.VMEM((3, rows, width), low_type),
            pltpu.VMEM((3, rows, width), low_type),
            pltpu.VMEM((3, units, features), low_type),
            pltpu.VMEM((2, 4, 2 * rows, width), low_type),
            pltpu.VMEM((2, 4, 2 * rows, width), low_type),
            pltpu.VMEM((4, 16, width), low_type),
            pltpu.VMEM((3, 2, 2 * rows, units), f32),
            pltpu.VMEM((3, 2, 2 * rows, units), low_type),
            pltpu.VMEM((3, 2, 2 * rows, units), low_type),
            pltpu.VMEM((2, 2 * rows, units), low_type),
            pltpu.VMEM((2, 2 * rows, units), low_type),
            pltpu.VMEM((2, 2 * rows, units), low_type),
            pltpu.VMEM((16, units), f32),
            pltpu.VMEM((16, units), f32),
            pltpu.VMEM((5, 8, 128), f32),
            pltpu.VMEM((5, 8, 128), f32),
            dma((3,)), dma((2, 3)), dma((2, 3)), dma((3,)), dma((3,)),
            dma((2, 4)), dma((2, 4)), dma((2, 2)), dma((2, 2)),
            dma((3, 2, 2)), dma((3, 2, 2)), dma(()), dma(()), dma((5,)), dma((5,)), dma((11,)),
            dma((2, 4)), dma((2, 4)), dma((4,)), dma((4,)), dma((3,)), dma((3,)),
        ],
        compiler_params=pltpu.CompilerParams(
            collective_id=0, has_side_effects=True, vmem_limit_bytes=62 * 1024 * 1024
        ),
        cost_estimate=pl.CostEstimate(
            flops=flops, bytes_accessed=3 * units * features * 2, transcendentals=0
        ),
    )(tokens, lm_grad, head_row, gate_weight, up_weight, down_weight, diff)


def kernel_body(tokens, gate_weight, up_weight, down_weight, reward_head, lm_grad, pair_index):
    rows, width = tokens.shape
    units, features = gate_weight.shape
    seq_total = lax.axis_size("gx")
    sequence = jnp.arange(128, dtype=jnp.int32)
    diff = (pair_index[:, 1:2] == sequence[None, :]).astype(jnp.float32) - (
        pair_index[:, 0:1] == sequence[None, :]
    ).astype(jnp.float32)
    diff = jnp.pad(diff, ((0, 8 - diff.shape[0]), (0, 0)))
    tok_all, low_all, hidden, gate_grad, up_grad, grad_tokens, reward_tile = forward_call(
        tokens, lm_grad, reward_head[None, :], gate_weight, up_weight, down_weight, diff
    )
    tok_all = tok_all.reshape(4 * rows, features)
    low_all = low_all.reshape(4 * rows, features)
    hidden = hidden.reshape(4 * rows, units)
    gate_grad = gate_grad.reshape(4 * rows, units)
    up_grad = up_grad.reshape(4 * rows, units)
    loss_scale = 1.0 / jnp.sqrt(jnp.float32(4 * rows))

    def weight_grad(left, right):
        return jnp.einsum("tf,td->fd", left, right, preferred_element_type=jnp.float32) * loss_scale

    return (
        grad_tokens,
        weight_grad(gate_grad, tok_all),
        weight_grad(up_grad, tok_all),
        weight_grad(hidden, low_all),
        reward_tile[0, :seq_total],
    )


def body(*args):
    sizes = tuple(lax.axis_size(axis) for axis in ("gx", "gy", "gz"))
    if sizes == (4, 4, 2) and args[0].shape[0] == SEQ_LEN:
        return kernel_body(*args)
    return permute_body(*args)


def solution(mesh):
    placed = (
        P("gx", ("gz", "gy")),
        P(("gy", "gx"), "gz"),
        P(("gy", "gx"), "gz"),
        P(("gy", "gx"), "gz"),
        P(("gz", "gy")),
        P("gx", ("gz", "gy")),
        P(),
    )
    return jax.shard_map(
        body,
        mesh=mesh,
        in_specs=placed,
        out_specs=(
            P("gx", ("gz", "gy")),
            P(("gy", "gx"), "gz"),
            P(("gy", "gx"), "gz"),
            P(("gy", "gx"), "gz"),
            P(),
        ),
        check_vma=False,
    )
```
